32 devices in a mesh: gx: 4 (over y, x), gy: 4 (over z), gz: 2 (over core).
Axes of the slice: x: 2, y: 2, z: 4, core: 2. Of those that a mesh axis runs over, the one named last changes fastest.
Arguments:
- orbitals: float32 [8, 64, 64, 256], P(None, 'gx', 'gy', 'gz'), may hold values from -7 to 7
- potential: float32 [64, 64, 256], P('gx', 'gy', 'gz'), may hold values from -2 to 1
- locked: bfloat16 [64, 64, 64, 256], P(None, 'gx', 'gy', 'gz'), may hold values from -160 to 160
- sphere_cell: int32 [4, 4, 2, 16384], P('gx', 'gy', 'gz'), may hold values from 0 to 32767
- sphere_owner: int32 [4, 4, 2, 16384], P('gx', 'gy', 'gz'), may hold values from 0 to 26
- sphere_atom: int32 [4, 4, 2, 16384], P('gx', 'gy', 'gz'), may hold values from 0 to 31
- sphere_profile: float32 [4, 4, 2, 9, 16384], P('gx', 'gy', 'gz'), may hold values from -1.2 to 1.2
- atom_strength: float32 [4, 4, 2, 32, 9], P('gx', 'gy', 'gz'), may hold values from -0.5 to 2
- atom_channels: int32 [4, 4, 2, 32], P('gx', 'gy', 'gz'), may hold values from 0 to 9, as said below
Outputs:
- projected: float32 [8, 64, 64, 256], P(None, 'gx', 'gy', 'gz')
The draws below stay inside these ranges and needn't reach their ends.
Inputs may be any that keep to these rules, and one draw needn't show every extreme that they name: `sphere_owner`: A code o stands for the domain (e, f, g) steps away along the three axes, o = 9 (e + 1) + 3 (f + 1) + (g + 1), with the grid's ends joined; every code occurs. `atom_channels`: each entry is 0, 1, 4 or 9; the first slot of every domain has 9.
All inputs are finite; a program needn't handle non-finite values.
Results may differ from the reference program's by a relative error of at most 0.0018.
Values sent between devices are 32-bit elements; how exact they have to be, the bound alone decides.
No kernel may reach another device: no remote copies, remote signals or barrier semaphores. Data moves between devices by JAX's collectives and lax.ppermute only.
A program may use at most 128 MiB of HBM per device.

```python
import jax
import jax.numpy as jnp
from jax import lax

CX = 16
CY = 16
CZ = 128
ATOM_DEV = 32
POINTS = 16384
ORBS = 8
LOCKED = 64
NPROJ = 9
CELLS = 32768
NX = 64
NY = 64
NZ = 256
N_GX = 4
N_GY = 4
N_GZ = 2


def unit_slab(key, position, slab):
    subkey = jax.random.fold_in(jax.random.fold_in(jax.random.fold_in(key, 11), position), slab)
    values = jnp.clip(jax.random.normal(subkey, (NY, NZ), jnp.float32), -5.0, 5.0)
    return values


def noise_slab(key, position, slab):
    subkey = jax.random.fold_in(jax.random.fold_in(jax.random.fold_in(key, 17), position), slab)
    values = jnp.clip(jax.random.normal(subkey, (NY, NZ), jnp.float32), -5.0, 5.0)
    return values


def slab_scale(slab):
    position_one = slab.astype(jnp.float32) / NX
    position_two = jnp.arange(NY, dtype=jnp.float32)[:, None] / NY
    position_three = jnp.arange(NZ, dtype=jnp.float32)[None, :] / NZ
    exponent = 0.6 * position_one + 0.2 * position_two + 0.2 * position_three
    return 10.0 ** exponent


def orbital_shape(slab):
    position_one = slab.astype(jnp.float32) / NX
    position_two = jnp.arange(NY, dtype=jnp.float32)[:, None] / NY
    position_three = jnp.arange(NZ, dtype=jnp.float32)[None, :] / NZ
    return 0.5 + position_one + 0.5 * position_two + 0.0 * position_three


def draw_locked(key, part):
    weights = 10.0 ** (0.5 * jax.random.uniform(jax.random.fold_in(key, 13), (LOCKED,), jnp.float32))
    offsets = jax.random.permutation(jax.random.fold_in(key, 29), LOCKED - 1)[:7].astype(jnp.int32) + 1
    blend = jax.random.uniform(jax.random.fold_in(key, 23), (LOCKED, 7), jnp.float32, -0.13, 0.13)
    rows = jnp.arange(LOCKED, dtype=jnp.int32)

    def single(slab):
        fields = lax.map(lambda position: unit_slab(key, position, slab), rows)
        total = fields + 0.4
        for member in range(7):
            partner = jnp.take(fields, (rows + offsets[member]) % LOCKED, axis=0)
            total = total + blend[:, member][:, None, None] * partner
        values = total * slab_scale(slab)[None] * weights[:, None, None]
        return jnp.clip(values, -160.0, 160.0).astype(jnp.bfloat16)
    stacked = lax.map(single, jnp.arange(NX, dtype=jnp.int32))
    return jnp.moveaxis(stacked, 0, 1)


def draw_orbitals(key, part):
    amplitude = jax.random.uniform(jax.random.fold_in(key, 37), (ORBS,), jnp.float32, 0.08, 0.16)

    def single(slab):
        shape_field = orbital_shape(slab)

        def one_orbital(position):
            values = 0.6 * unit_slab(key, position, slab) + 0.8 * noise_slab(key, position, slab)
            values = values + amplitude[position] * shape_field
            return jnp.clip(values, -7.0, 7.0)
        return lax.map(one_orbital, jnp.arange(ORBS, dtype=jnp.int32))
    stacked = lax.map(single, jnp.arange(NX, dtype=jnp.int32))
    return jnp.moveaxis(stacked, 0, 1)


def draw_sphere_profile(key, part):
    subkey = jax.random.fold_in(key, 31)
    shape = (N_GX, N_GY, N_GZ, NPROJ, POINTS)
    values = 0.2 * jnp.clip(jax.random.normal(subkey, shape, jnp.float32), -6.0, 6.0)
    channel = jnp.arange(NPROJ, dtype=jnp.int32)[None, None, None, :, None]
    return jnp.where(channel == 0, jnp.abs(values), values)


def draw_atom_channels(key, part):
    level_pick = jax.random.randint(jax.random.fold_in(key, 19), (N_GX, N_GY, N_GZ, ATOM_DEV), 0, 4)
    levels = jnp.array([0, 1, 4, 9], jnp.int32)
    counts = jnp.take(levels, level_pick)
    return counts.at[:, :, :, 0].set(9)


def touch_ends(entries, rng, smallest, high):
    dims = entries.shape
    place = [jax.random.randint(jax.random.fold_in(rng, axis), (), 0, dims[axis]) for axis in range(len(dims))]
    entries = entries.at[tuple(place)].set(smallest)
    longest = dims.index(max(dims))
    place[longest] = (place[longest] + 1) % dims[longest]
    return entries.at[tuple(place)].set(high)


def shard_levels(own_key, dims, shards, least, largest):
    level = 1.0
    for axis_at, parts in shards:
        heights = jax.random.uniform(jax.random.fold_in(jax.random.fold_in(own_key, 6), axis_at), (parts,), jnp.float32, least / len(shards), largest / len(shards))
        level = level * jnp.repeat(jnp.exp(heights), dims[axis_at] // parts).reshape((-1,) + (1,) * (len(dims) - 1 - axis_at))
    return level


def setup_inputs(seed: int = 0) -> dict:
    arg_keys = jax.random.split(jax.random.key(seed), 10)
    return {
        "orbitals": draw_orbitals(jax.random.fold_in(arg_keys[9], 71), 0),
        "potential": jnp.clip(-2.0 + 3.0 * jax.random.uniform(arg_keys[1], (NX, NY, NZ), jnp.float32) ** shard_levels(arg_keys[1], (NX, NY, NZ), ((0, 4), (1, 4), (2, 2)), -0.2, 0.2), -2.0, 1.0),
        "locked": draw_locked(jax.random.fold_in(arg_keys[9], 71), 0),
        "sphere_cell": touch_ends(jax.random.randint(arg_keys[3], (N_GX, N_GY, N_GZ, POINTS), 0, CELLS), jax.random.fold_in(arg_keys[3], 1), 0, CELLS - 1).astype(jnp.int32),
        "sphere_owner": touch_ends(jax.random.randint(arg_keys[4], (N_GX, N_GY, N_GZ, POINTS), 0, 27), jax.random.fold_in(arg_keys[4], 1), 0, 26).astype(jnp.int32),
        "sphere_atom": touch_ends(jax.random.randint(arg_keys[5], (N_GX, N_GY, N_GZ, POINTS), 0, ATOM_DEV), jax.random.fold_in(arg_keys[5], 1), 0, ATOM_DEV - 1).astype(jnp.int32),
        "sphere_profile": draw_sphere_profile(jax.random.fold_in(arg_keys[9], 71), 0),
        "atom_strength": jnp.clip(-0.5 + 2.5 * jax.random.uniform(arg_keys[7], (N_GX, N_GY, N_GZ, ATOM_DEV, NPROJ), jnp.float32) ** shard_levels(arg_keys[7], (N_GX, N_GY, N_GZ, ATOM_DEV, NPROJ), ((0, 4), (1, 4), (2, 2)), -0.2, 0.2), -0.5, 2.0),
        "atom_channels": draw_atom_channels(jax.random.fold_in(arg_keys[9], 71), 0),
    }


STENCIL_WEIGHTS = (-205.0 / 72.0, 8.0 / 5.0, -1.0 / 5.0, 8.0 / 315.0, -1.0 / 560.0)

def slot_onehot(owners, atom_ids, atom_slots):
    slot_ids = owners * atom_slots + atom_ids
    labels = jnp.arange(27 * atom_slots, dtype=jnp.int32)
    return (labels[:, None] == slot_ids[None, :]).astype(jnp.float32)

def gather_slots(flat_orbitals, cell_index, onehot, profile):
    values = jnp.take(flat_orbitals, cell_index, axis=1)
    products = (profile[:, None, :] * values[None, :, :]).reshape(-1, cell_index.shape[0])
    return lax.dot_general(onehot.astype(jnp.float32), products.astype(jnp.float32), (((1,), (1,)), ((), ())), precision=lax.Precision.HIGHEST, preferred_element_type=jnp.float32)

def spread_terms(returned, cell_index, onehot, profile, orbit_count, cell_count):
    picked = lax.dot_general(returned.astype(jnp.float32), onehot.astype(jnp.float32), (((0,), (0,)), ((), ())), precision=lax.Precision.HIGHEST, preferred_element_type=jnp.float32)
    picked = picked.reshape(profile.shape[0], orbit_count, cell_index.shape[0])
    spread = jnp.sum(profile[:, None, :] * picked, axis=0)
    return jnp.zeros((orbit_count, cell_count), jnp.float32).at[:, cell_index].add(spread)

def locked_solve(gram_matrix, correlation):
    factor = jnp.linalg.cholesky(gram_matrix)
    middle = lax.linalg.triangular_solve(factor, correlation, left_side=True, lower=True)
    return lax.linalg.triangular_solve(factor, middle, left_side=True, lower=True, transpose_a=True)

def to_blocks(grid_field):
    leading = grid_field.shape[0]
    shaped = grid_field.reshape(leading, N_GX, CX, N_GY, CY, N_GZ, CZ)
    return shaped.transpose(1, 3, 5, 0, 2, 4, 6).reshape(N_GX * N_GY * N_GZ, leading, CX * CY * CZ)

def from_blocks(blocks):
    leading = blocks.shape[1]
    shaped = blocks.reshape(N_GX, N_GY, N_GZ, leading, CX, CY, CZ)
    return shaped.transpose(3, 0, 4, 1, 5, 2, 6).reshape(leading, N_GX * CX, N_GY * CY, N_GZ * CZ)

def reference(orbitals, potential, locked, sphere_cell, sphere_owner, sphere_atom, sphere_profile, atom_strength, atom_channels):
    domains = N_GX * N_GY * N_GZ
    cell_count = CX * CY * CZ
    laplace = 3.0 * STENCIL_WEIGHTS[0] * orbitals
    for dimension in (1, 2, 3):
        for distance in range(1, 5):
            laplace = laplace + STENCIL_WEIGHTS[distance] * (jnp.roll(orbitals, distance, dimension) + jnp.roll(orbitals, -distance, dimension))
    local_part = -0.5 * laplace + potential[None] * orbitals
    cells_flat = sphere_cell.reshape(domains, POINTS)
    owners_flat = sphere_owner.reshape(domains, POINTS)
    atoms_flat = sphere_atom.reshape(domains, POINTS)
    profile_flat = sphere_profile.reshape(domains, NPROJ, POINTS)

    def partial_sums(inputs):
        flat_orbitals, cell_index, owners, atom_ids, profile = inputs
        onehot = slot_onehot(owners, atom_ids, ATOM_DEV)
        return gather_slots(flat_orbitals, cell_index, onehot, profile)
    slot_sums = lax.map(partial_sums, (to_blocks(orbitals), cells_flat, owners_flat, atoms_flat, profile_flat))
    slot_sums = slot_sums.reshape(N_GX, N_GY, N_GZ, 3, 3, 3, ATOM_DEV * NPROJ * ORBS)
    coefficient = jnp.zeros((N_GX, N_GY, N_GZ, ATOM_DEV * NPROJ * ORBS), jnp.float32)
    for neighbour in range(27):
        step_one = neighbour // 9 - 1
        step_two = neighbour // 3 % 3 - 1
        step_three = neighbour % 3 - 1
        coefficient = coefficient + jnp.roll(slot_sums[:, :, :, step_one + 1, step_two + 1, step_three + 1], (step_one, step_two, step_three), (0, 1, 2))
    active = jnp.arange(NPROJ, dtype=jnp.int32)[None, None, None, None, :] < atom_channels[..., None]
    strength = jnp.where(active, atom_strength, 0.0)
    weighted = coefficient.reshape(N_GX, N_GY, N_GZ, ATOM_DEV, NPROJ, ORBS) * strength[..., None]
    weighted = weighted.reshape(N_GX, N_GY, N_GZ, ATOM_DEV * NPROJ * ORBS)
    shifted = []
    for neighbour in range(27):
        step_one = neighbour // 9 - 1
        step_two = neighbour // 3 % 3 - 1
        step_three = neighbour % 3 - 1
        shifted.append(jnp.roll(weighted, (-step_one, -step_two, -step_three), (0, 1, 2)))
    returned = jnp.stack(shifted, axis=3).reshape(domains, 27 * ATOM_DEV, NPROJ * ORBS)

    def spread(inputs):
        back, cell_index, owners, atom_ids, profile = inputs
        onehot = slot_onehot(owners, atom_ids, ATOM_DEV)
        return spread_terms(back, cell_index, onehot, profile, ORBS, cell_count)
    nonlocal_blocks = lax.map(spread, (returned, cells_flat, owners_flat, atoms_flat, profile_flat))
    applied = local_part + from_blocks(nonlocal_blocks)
    rounded = applied.astype(jnp.bfloat16)

    def accumulate(running, position):
        gram_matrix, correlation = running
        locked_slab = lax.dynamic_slice_in_dim(locked, position, 1, 1).reshape(LOCKED, NY * NZ).astype(jnp.float32)
        applied_slab = lax.dynamic_slice_in_dim(rounded, position, 1, 1).reshape(ORBS, NY * NZ).astype(jnp.float32)
        gram_matrix = gram_matrix + lax.dot_general(locked_slab.astype(jnp.float32), locked_slab.astype(jnp.float32), (((1,), (1,)), ((), ())), precision=lax.Precision.HIGHEST, preferred_element_type=jnp.float32)
        correlation = correlation + lax.dot_general(locked_slab.astype(jnp.float32), applied_slab.astype(jnp.float32), (((1,), (1,)), ((), ())), precision=lax.Precision.HIGHEST, preferred_element_type=jnp.float32)
        return ((gram_matrix, correlation), None)
    start = (jnp.zeros((LOCKED, LOCKED), jnp.float32), jnp.zeros((LOCKED, ORBS), jnp.float32))
    (gram_matrix, correlation), unused = lax.scan(accumulate, start, jnp.arange(NX, dtype=jnp.int32))
    mixing = locked_solve(gram_matrix, correlation).astype(jnp.bfloat16)

    def correct(position):
        locked_slab = lax.dynamic_slice_in_dim(locked, position, 1, 1).reshape(LOCKED, NY * NZ)
        return lax.dot_general(mixing.astype(jnp.float32), locked_slab.astype(jnp.float32), (((0,), (0,)), ((), ())), preferred_element_type=jnp.float32)
    corrections = lax.map(correct, jnp.arange(NX, dtype=jnp.int32))
    correction = jnp.moveaxis(corrections, 0, 1).reshape(ORBS, NX, NY, NZ)
    return applied - correction
```

```python
import functools

import jax
import jax.numpy as jnp
from jax import lax
from jax.experimental import pallas as pl
from jax.experimental.pallas import tpu as pltpu
from jax.sharding import PartitionSpec as P

STENCIL_WEIGHTS = (-205.0 / 72.0, 8.0 / 5.0, -1.0 / 5.0, 8.0 / 315.0, -1.0 / 560.0)
F32, BF16 = jnp.float32, jnp.bfloat16
NT = (((1,), (1,)), ((), ()))
VMEM = pl.BlockSpec(memory_space=pltpu.VMEM)
MIB = 1024 * 1024
COLLECT_TILE = 4096
SPREAD_TILE = 4096
COLLECT_SUB = 1024
SPREAD_SUB = 1024
FLAT = ("gx", "gy")


def params(mebibytes=36):
    return pltpu.CompilerParams(vmem_limit_bytes=mebibytes * MIB)


def shifted(block, axis, step):
    count = lax.axis_size(axis)
    return lax.ppermute(block, axis, [(i, (i + step) % count) for i in range(count)])


def split_pieces(values):
    upper = values.astype(BF16).astype(F32)
    return upper, values - upper


def turn_kernel(orb_ref, rows_ref, table_ref, ends_ref, low_ref, high_ref, left_ref, right_ref):
    span_one, span_two, orbits, lanes = rows_ref.shape
    count = span_one * span_two
    half = count // 2
    lane = lax.broadcasted_iota(jnp.int32, (orbits, lanes), 1)
    packed = [None] * span_one
    for pair in range(half // 2):
        for side in range(2):
            found = []
            for r in (side * half + 2 * pair, side * half + 2 * pair + 1):
                value = orb_ref[pl.ds(r, orbits, stride=count), :]
                i, j = divmod(r, span_two)
                rows_ref[i, j] = value
                if i < 4:
                    low_ref[i, j] = value
                if i >= span_one - 4:
                    high_ref[i + 4 - span_one, j] = value
                if j < 4:
                    left_ref[i, j] = value
                if j >= span_two - 4:
                    right_ref[i, j + 4 - span_two] = value
                found.append(value)
                turned = pltpu.roll(value, (4 + 8 * j) % lanes, 1)
                packed[i] = turned if j == 0 else jnp.where(lane >= 8 * j, turned, packed[i])
                if j == span_two - 1:
                    ends_ref[i] = packed[i]
            upper, lower = split_pieces(jnp.concatenate(found, axis=0))
            low, high = pair * 2 * orbits, (pair + 1) * 2 * orbits
            for piece, base in ((upper, 0), (lower, 256)):
                base = base + side * 128
                table_ref[low:high, base : base + 128] = piece.astype(BF16)


def turn(orbitals):
    orbits, span_one, span_two, lanes = orbitals.shape
    count = span_one * span_two
    return pl.pallas_call(
        turn_kernel,
        out_shape=(
            jax.ShapeDtypeStruct((span_one, span_two, orbits, lanes), F32),
            jax.ShapeDtypeStruct((count // 2 * orbits, 512), BF16),
            jax.ShapeDtypeStruct((span_one, orbits, lanes), F32),
            jax.ShapeDtypeStruct((4, span_two, orbits, lanes), F32),
            jax.ShapeDtypeStruct((4, span_two, orbits, lanes), F32),
            jax.ShapeDtypeStruct((span_one, 4, orbits, lanes), F32),
            jax.ShapeDtypeStruct((span_one, 4, orbits, lanes), F32),
        ),
        in_specs=[VMEM],
        out_specs=(VMEM,) * 7,
        compiler_params=params(),
        cost_estimate=pl.CostEstimate(flops=2**26, bytes_accessed=2**23, transcendentals=0),
        name="turn",
    )(orbitals.reshape(orbits * count, lanes))


def cut(value, count):
    assert count & (count - 1) == 0
    return lax.shift_right_logical(value, jnp.int32(count.bit_length() - 1)), value & (count - 1)


def cell_parts(code, cells, half):
    row, lane = cut(code & (cells - 1), 128)
    group, row = cut(row, half)
    return group, row, lane


def label_parts(code, cells, atom_slots, classes):
    owner, atom = cut(cut(code, cells)[0], atom_slots)
    across = lax.shift_right_logical(owner * 43, jnp.int32(7))
    along = owner - 3 * across
    if classes == 1:
        along = jnp.zeros_like(along)
    elif classes == 2:
        along = jnp.where(along == 1, 0, 1)
    return along * 9 + across, atom


def pair_onehot(outer, outer_count, inner, inner_count, padded=0):
    tile = outer.shape[1]
    rows = lax.broadcasted_iota(jnp.int32, (inner_count, tile), 0)
    block = jnp.where(rows == inner, 1.0, 0.0)
    wide = jnp.broadcast_to(outer, (inner_count, tile))
    parts = [jnp.where(wide == at, block, 0.0) for at in range(outer_count)]
    if padded > outer_count * inner_count:
        parts.append(jnp.zeros((padded - outer_count * inner_count, tile), F32))
    return jnp.concatenate(parts, axis=0).astype(BF16)


def collect_kernel(table_ref, code_ref, profile_ref, *refs, classes, atom_slots):
    out_refs, picked_refs, total = refs[:classes], refs[classes : classes + 2], refs[-1]
    step = pl.program_id(0)
    orbits = 8
    half = table_ref.shape[0] // orbits
    cells = half * 2 * 128
    channels = profile_ref.shape[0]
    subs = COLLECT_TILE // COLLECT_SUB

    def pick(at, target):
        group, _, lane = cell_parts(code_ref[:, pl.ds(pl.multiple_of(at, COLLECT_SUB), COLLECT_SUB)], cells, half)
        spot = pair_onehot(group, 2, lane, 128)
        target[...] = jnp.dot(
            table_ref[...], jnp.concatenate([spot, spot], axis=0), preferred_element_type=F32
        )

    def add(at, picked, live=None):
        here = pl.ds(pl.multiple_of(at, COLLECT_SUB), COLLECT_SUB)
        code = code_ref[:, here]
        wide_row = jnp.broadcast_to(cell_parts(code, cells, half)[1], (orbits, COLLECT_SUB))
        if live is not None:
            wide_row = jnp.where(live, wide_row, half)
        values = jnp.zeros((orbits, COLLECT_SUB), F32)
        for r in range(half):
            values = jnp.where(wide_row == r, picked[r * orbits : (r + 1) * orbits, :], values)
        products = jnp.concatenate(
            [profile_ref[p, :, here] * values for p in range(channels)], axis=0
        )
        pieces = jnp.concatenate(split_pieces(products), axis=0).astype(BF16)
        outer, inner = label_parts(code, cells, atom_slots, classes)
        onehot = pair_onehot(outer, 9 * classes, inner, atom_slots)
        return lax.dot_general(onehot, pieces, NT, preferred_element_type=F32)

    @pl.when(step == 0)
    def _():
        total[...] = jnp.zeros_like(total)

    start = step * COLLECT_TILE
    part = None
    for s in range(subs):
        pick(start + s * COLLECT_SUB, picked_refs[s % 2])
        if s == 0:
            part = add(jnp.maximum(start - COLLECT_SUB, 0), picked_refs[1], step > 0)
        else:
            part = part + add(start + (s - 1) * COLLECT_SUB, picked_refs[(s - 1) % 2])
    total[...] += part

    @pl.when(step == pl.num_programs(0) - 1)
    def _():
        total[...] += add(start + (subs - 1) * COLLECT_SUB, picked_refs[(subs - 1) % 2])
        rows, width = out_refs[0].shape
        for c, out_ref in enumerate(out_refs):
            block = total[c * rows : (c + 1) * rows]
            out_ref[...] = block[:, :width] + block[:, width:]


def collect(table, code, profile, classes, atom_slots):
    points = code.shape[1]
    channels = profile.shape[0]
    rows, width = 9 * atom_slots, channels * 8
    return pl.pallas_call(
        functools.partial(collect_kernel, classes=classes, atom_slots=atom_slots),
        grid=(points // COLLECT_TILE,),
        out_shape=(jax.ShapeDtypeStruct((rows, width), F32),) * classes,
        in_specs=[VMEM] * 3,
        out_specs=(VMEM,) * classes,
        scratch_shapes=[
            pltpu.VMEM((table.shape[0], COLLECT_SUB), F32),
            pltpu.VMEM((table.shape[0], COLLECT_SUB), F32),
            pltpu.VMEM((rows * classes, 2 * width), F32),
        ],
        compiler_params=params(),
        cost_estimate=pl.CostEstimate(
            flops=2 * points * table.shape[0] * 512, bytes_accessed=2**21, transcendentals=0
        ),
        name="collect",
    )(table, code, profile)


def fold_kernel(*refs, rows):
    total = None
    for ref in refs[:-1]:
        for at in range(ref.shape[0] // rows):
            block = ref[at * rows : (at + 1) * rows]
            total = block if total is None else total + block
    for at in range(refs[-1].shape[0] // rows):
        refs[-1][at * rows : (at + 1) * rows] = total


def fold(stacks, rows, copies):
    return pl.pallas_call(
        functools.partial(fold_kernel, rows=rows),
        out_shape=jax.ShapeDtypeStruct((rows * copies, stacks[0].shape[1]), F32),
        in_specs=[VMEM] * len(stacks),
        out_specs=VMEM,
        compiler_params=params(),
        name="fold",
    )(*stacks)


def summed(shares):
    if len(shares) == 1:
        return (lax.psum(shares[0], ("gx", "gy", "gz")),)
    mine, other = shares
    rows = mine.shape[0]
    copies = fold((mine, shifted(other, "gz", 1)), rows, lax.axis_size(FLAT))
    mine = fold((lax.all_to_all(copies, FLAT, 0, 0, tiled=True),), rows, 1)
    return mine, shifted(mine, "gz", 1)


def merge_kernel(*refs, addends):
    total = refs[0][...]
    for ref in refs[1:addends]:
        total = total + ref[...]
    out_refs = refs[addends:]
    rows = out_refs[0].shape[0]
    for at, out_ref in enumerate(out_refs):
        out_ref[...] = total[at * rows : (at + 1) * rows]


def merge(addends, pieces):
    rows, width = addends[0].shape
    return pl.pallas_call(
        functools.partial(merge_kernel, addends=len(addends)),
        out_shape=(jax.ShapeDtypeStruct((rows // pieces, width), F32),) * pieces,
        in_specs=[VMEM] * len(addends),
        out_specs=(VMEM,) * pieces,
        compiler_params=params(),
        name="merge",
    )(*addends)


def weigh_kernel(one_ref, two_ref, three_ref, strength_ref, out_ref):
    out_ref[...] = (one_ref[...] + two_ref[...] + three_ref[...]) * strength_ref[...]


def weigh(one, two, three, strength):
    return pl.pallas_call(
        weigh_kernel,
        out_shape=jax.ShapeDtypeStruct(strength.shape, F32),
        in_specs=[VMEM] * 4,
        out_specs=VMEM,
        compiler_params=params(),
        name="weigh",
    )(one, two, three, strength)


def stack_kernel(*refs):
    rows = refs[0].shape[0]
    for at, ref in enumerate(refs[:-1]):
        refs[-1][at * rows : (at + 1) * rows] = ref[...]


def stack(blocks):
    rows, width = blocks[0].shape
    return pl.pallas_call(
        stack_kernel,
        out_shape=jax.ShapeDtypeStruct((rows * len(blocks), width), F32),
        in_specs=[VMEM] * len(blocks),
        out_specs=VMEM,
        compiler_params=params(),
        name="stack",
    )(*blocks)


def stencil_kernel(rows_ref, below_ref, above_ref, left_ref, right_ref, near_ref, far_ref, pot_ref, out_ref, tall, pair):
    span_one, span_two, orbits, lanes = rows_ref.shape
    rows = span_one * span_two * orbits
    weights = [-0.5 * w for w in STENCIL_WEIGHTS]
    tall[0:4] = below_ref[...]
    tall[4 : 4 + span_one] = rows_ref[...]
    tall[4 + span_one : 8 + span_one] = above_ref[...]
    source = lax.broadcasted_iota(jnp.int32, (lanes, lanes), 0)
    target = lax.broadcasted_iota(jnp.int32, (lanes, lanes), 1)
    ghost = jnp.where(source % 8 < 4, source % 8 - 4, source % 8 - 4 + lanes)

    def band(gap):
        found = jnp.zeros((lanes, lanes), F32)
        for d in range(1, 5):
            found = jnp.where(jnp.abs(gap) == d, weights[d], found)
        return split_pieces(found)

    main_upper, main_lower = band(source - target)
    ends_upper, ends_lower = band(ghost - target)
    ends = jnp.where(source < 16, ends_upper, jnp.where(source < 24, ends_lower, 0.0))
    first = jnp.concatenate([main_upper, main_upper], axis=0).astype(BF16)
    second = jnp.concatenate([main_lower, ends], axis=0).astype(BF16)
    lane = lax.broadcasted_iota(jnp.int32, (orbits, lanes), 1)

    def prepare(i, carry):
        upper, lower = split_pieces(rows_ref[i].reshape(span_two * orbits, lanes))
        base = pl.multiple_of(i * span_two * orbits, span_two * orbits)
        pair[pl.ds(base, span_two * orbits), :lanes] = lower.astype(BF16)
        pair[pl.ds(base, span_two * orbits), lanes : 2 * lanes] = upper.astype(BF16)
        upper, lower = split_pieces(jnp.where(lane % 8 < 4, near_ref[i], far_ref[i]))
        found = []
        for j in range(span_two):
            one = pltpu.roll(upper, (lanes - 8 * j) % lanes, 1)
            two = pltpu.roll(lower, (lanes + 8 - 8 * j) % lanes, 1)
            three = pltpu.roll(upper, (lanes + 16 - 8 * j) % lanes, 1)
            found.append(jnp.where(lane < 8, one, jnp.where(lane < 16, two, three)))
        pair[pl.ds(base, span_two * orbits), 2 * lanes :] = jnp.concatenate(
            found, axis=0
        ).astype(BF16)
        return carry

    lax.fori_loop(0, span_one, prepare, 0)
    along = jnp.dot(pair[:, : 2 * lanes], first, preferred_element_type=F32)
    along = along + jnp.dot(pair[:, lanes:], second, preferred_element_type=F32)
    out_ref[...] = along.reshape(out_ref.shape)

    def plane(i, carry):
        line = [left_ref[i, j] for j in range(4)]
        line += [rows_ref[i, j] for j in range(span_two)]
        line += [right_ref[i, j] for j in range(4)]
        for j in range(span_two):
            acc = out_ref[i, j] + line[4 + j] * (3.0 * weights[0] + pot_ref[i, j : j + 1, :])
            for d in range(1, 5):
                four = tall[i + 4 + d, j] + tall[i + 4 - d, j]
                four = four + (line[4 + j + d] + line[4 + j - d])
                acc = acc + weights[d] * four
            out_ref[i, j] = acc
        return carry

    lax.fori_loop(0, span_one, plane, 0)


def stencil(rows, below, above, left, right, near, far, potential):
    span_one, span_two, orbits, lanes = rows.shape
    return pl.pallas_call(
        stencil_kernel,
        out_shape=jax.ShapeDtypeStruct(rows.shape, F32),
        in_specs=[VMEM] * 8,
        out_specs=VMEM,
        scratch_shapes=[
            pltpu.VMEM((span_one + 8, span_two, orbits, lanes), F32),
            pltpu.VMEM((span_one * span_two * orbits, 3 * lanes), BF16),
        ],
        compiler_params=params(),
        cost_estimate=pl.CostEstimate(flops=2**24, bytes_accessed=2**22, transcendentals=0),
        name="stencil",
    )(rows, below, above, left, right, near, far, potential)


def spread_kernel(*refs, classes, atom_slots):
    back_refs = refs[:classes]
    code_ref, profile_ref, local_ref, locked_ref, gram_ref = refs[classes : classes + 5]
    out_ref, *sums_refs = refs[classes + 5 : -5]
    turned, weights_a, weights_b, total, corr_ref = refs[-5:]
    step = pl.program_id(0)
    orbits = 8
    half = total.shape[0] // orbits
    groups = total.shape[1] // 128
    cells = half * groups * 128
    locked_count = gram_ref.shape[0]
    channels = profile_ref.shape[0]
    width = back_refs[0].shape[1]
    weights = (weights_a, weights_b)
    subs = SPREAD_TILE // SPREAD_SUB

    @pl.when(step == 0)
    def _():
        whole = jnp.concatenate([ref[...] for ref in back_refs], axis=0)
        pad = turned.shape[1] - whole.shape[0]
        whole = jnp.concatenate([whole, jnp.zeros((pad, width), F32)], axis=0)
        whole = jnp.concatenate([whole, jnp.zeros((whole.shape[0], 128 - width), F32)], axis=1)
        flipped = whole.T[:width]
        turned[...] = jnp.concatenate(split_pieces(flipped), axis=0).astype(BF16)
        total[...] = jnp.zeros_like(total)

    def weigh_points(at, target):
        here = pl.ds(at, SPREAD_SUB)
        code = code_ref[:, here]
        outer, inner = label_parts(code, cells, atom_slots, classes)
        onehot = pair_onehot(outer, 9 * classes, inner, atom_slots, turned.shape[1])
        picked = jnp.dot(turned[...], onehot, preferred_element_type=F32)
        spread = jnp.zeros((orbits, SPREAD_SUB), F32)
        for p in range(channels):
            low, high = p * orbits, width + p * orbits
            term = picked[low : low + orbits] + picked[high : high + orbits]
            spread = spread + profile_ref[p, :, here] * term
        upper, lower = split_pieces(spread)
        wide_row = jnp.broadcast_to(cell_parts(code, cells, half)[1], (orbits, SPREAD_SUB))
        for pair in range(half // 2):
            first, second = wide_row == 2 * pair, wide_row == 2 * pair + 1
            for place, piece in enumerate((upper, lower)):
                both = jnp.concatenate(
                    [jnp.where(first, piece, 0.0), jnp.where(second, piece, 0.0)], axis=0
                )
                target[pair * 16 : (pair + 1) * 16, place * SPREAD_SUB : (place + 1) * SPREAD_SUB] = both.astype(BF16)

    def scatter(at, source):
        group, _, lane = cell_parts(code_ref[:, pl.ds(at, SPREAD_SUB)], cells, half)
        spot = pair_onehot(group, groups, lane, 128)
        return lax.dot_general(
            source[...], jnp.concatenate([spot, spot], axis=1), NT, preferred_element_type=F32
        )

    part = None
    for s in range(subs + 1):
        at = step * SPREAD_TILE + s * SPREAD_SUB
        if s < subs:
            weigh_points(pl.multiple_of(at, SPREAD_SUB), weights[s % 2])
        if s > 0:
            term = scatter(pl.multiple_of(at - SPREAD_SUB, SPREAD_SUB), weights[(s - 1) % 2])
            part = term if part is None else part + term
    total[...] += part

    @pl.when(step == pl.num_programs(0) - 1)
    def _():
        rows = half * orbits
        for g in range(groups):
            there = slice(g * rows, (g + 1) * rows)
            out_ref[there] = total[:, g * 128 : (g + 1) * 128] + local_ref[there]
        corr_ref[...] = jnp.zeros_like(corr_ref)
        chunk = 32

        def add(c, carry):
            base = pl.multiple_of(c * chunk * orbits, 128)
            strip = out_ref[pl.ds(base, chunk * orbits), :]
            strip = jnp.concatenate(
                [strip[m * orbits : (m + 1) * orbits] for m in range(chunk)], axis=1
            ).astype(BF16)
            held = locked_ref[:, pl.ds(pl.multiple_of(c * chunk * 128, 128), chunk * 128)]
            corr_ref[...] += lax.dot_general(strip, held, NT, preferred_element_type=F32)
            return carry

        lax.fori_loop(0, groups * half // chunk, add, 0)
        side = locked_count // 2
        corr, gram = corr_ref[...], gram_ref[...]
        rest = jnp.zeros((side - 2 * orbits, side), F32)
        sums = jnp.concatenate(
            [
                gram[:side, :side],
                gram[side:, :side],
                gram[side:, side:],
                jnp.concatenate([corr[:, :side], corr[:, side:], rest], axis=0),
            ],
            axis=1,
        )
        if len(sums_refs) == 1:
            sums_refs[0][...] = sums
        else:
            middle = sums.shape[0] // 2
            first = lax.axis_index("gz") == 0
            sums_refs[0][...] = jnp.where(first, sums[:middle], sums[middle:])
            sums_refs[1][...] = jnp.where(first, sums[middle:], sums[:middle])


def spread(backs, code, profile, local, locked_flat, gram, atom_slots):
    classes = len(backs)
    points = code.shape[1]
    channels = profile.shape[0]
    labels = 9 * classes * atom_slots
    padded = (labels + 127) // 128 * 128
    rows = local.shape[0] // 4
    locked_count = gram.shape[0]
    shares = 2 if classes == 2 else 1
    sums = jax.ShapeDtypeStruct((locked_count // 2 // shares, 2 * locked_count), F32)
    return pl.pallas_call(
        functools.partial(spread_kernel, classes=classes, atom_slots=atom_slots),
        grid=(points // SPREAD_TILE,),
        out_shape=(jax.ShapeDtypeStruct(local.shape, F32),) + (sums,) * shares,
        in_specs=[VMEM] * (classes + 5),
        out_specs=(VMEM,) * (1 + shares),
        scratch_shapes=[
            pltpu.VMEM((2 * channels * 8, padded), BF16),
            pltpu.VMEM((rows, 2 * SPREAD_SUB), BF16),
            pltpu.VMEM((rows, 2 * SPREAD_SUB), BF16),
            pltpu.VMEM((rows, 512), F32),
            pltpu.VMEM((8, locked_count), F32),
        ],
        compiler_params=params(),
        cost_estimate=pl.CostEstimate(
            flops=2 * points * rows * 1024, bytes_accessed=2**23, transcendentals=0
        ),
        name="spread",
    )(*backs, code, profile, local, locked_flat, gram)


def solve_gram(gram):
    size = gram.shape[0]
    wide = (8, 2 * size)
    rows = lax.broadcasted_iota(jnp.int32, (size, size), 0)
    lanes = lax.broadcasted_iota(jnp.int32, (size, size), 1)
    both = jnp.concatenate([jnp.where(rows == lanes, 1.0, 0.0), gram], axis=1)
    blocks = [both[8 * b : 8 * b + 8] for b in range(size // 8)]
    place = lax.broadcasted_iota(jnp.int32, wide, 0)
    scaled = []
    for k in range(0, size, 2):
        b, s = divmod(k, 8)
        last = s + 2 == 8
        one = {
            c: jnp.broadcast_to(blocks[c][:, size + k : size + k + 1], wide)
            for c in range(b, size // 8)
        }
        two = {
            c: jnp.broadcast_to(blocks[c][:, size + k + 1 : size + k + 2], wide)
            for c in range(b, size // 8)
        }
        corner, side, end = one[b][s : s + 1], two[b][s : s + 1], two[b][s + 1 : s + 2]
        first, second = blocks[b][s : s + 1], blocks[b][s + 1 : s + 2]
        factor = 1.0 / (corner * end - side * side)
        upper = (end * first - side * second) * factor
        lower = (corner * second - side * first) * factor
        if s == 0:
            scaled.append(jnp.broadcast_to(upper, wide))
        else:
            scaled[b] = jnp.where(place == s, upper, scaled[b])
        scaled[b] = jnp.where(place == s + 1, lower, scaled[b])
        for c in range(b + 1 if last else b, size // 8):
            amount = one[c] * upper + two[c] * lower
            if c == b:
                amount = jnp.where(place > s + 1, amount, 0.0)
            blocks[c] = blocks[c] - amount
    return jnp.concatenate(blocks, axis=0), jnp.concatenate(scaled, axis=0)


def finish_kernel(applied_ref, locked_ref, *refs):
    *sums_refs, out_ref, lines, sent = refs
    orbits, locked_count = out_ref.shape[0], locked_ref.shape[0]
    parts = sent.shape[0]
    block = out_ref.shape[1] // parts
    sums = sums_refs[0][...]
    if len(sums_refs) == 2:
        first = lax.axis_index("gz") == 0
        other = sums_refs[1][...]
        sums = jnp.concatenate(
            [jnp.where(first, sums, other), jnp.where(first, other, sums)], axis=0
        )
    side = locked_count // 2
    across = sums[:, side : 2 * side]
    corr = sums[:, 3 * side :]
    corr = jnp.concatenate([corr[:orbits], corr[orbits : 2 * orbits]], axis=1)
    gram = jnp.concatenate(
        [
            jnp.concatenate([sums[:, :side], across.T], axis=1),
            jnp.concatenate([across, sums[:, 2 * side : 3 * side]], axis=1),
        ],
        axis=0,
    )
    upper, scaled = solve_gram(gram)
    middle = lax.dot_general(
        corr,
        scaled[:, :locked_count],
        NT,
        precision=lax.Precision.HIGHEST,
        preferred_element_type=F32,
    )
    mixing = jnp.dot(
        middle,
        upper[:, :locked_count],
        precision=lax.Precision.HIGHEST,
        preferred_element_type=F32,
    ).astype(BF16)

    copies = []
    for part in range(parts):
        cells = slice(part * block * 128, (part + 1) * block * 128)
        amount = jnp.dot(mixing, locked_ref[:, cells], preferred_element_type=F32)
        for r in range(block):
            row = part * block + r
            lines[part, pl.ds(r, orbits, stride=block), :] = (
                applied_ref[row * orbits : (row + 1) * orbits, :] - amount[:, r * 128 : (r + 1) * 128]
            )
        for n in range(orbits):
            copy = pltpu.make_async_copy(
                lines.at[part, pl.ds(n * block, block)],
                out_ref.at[n, pl.ds(part * block, block)],
                sent.at[part, n],
            )
            copy.start()
            copies.append(copy)
    for copy in copies:
        copy.wait()


def finish(applied, locked_flat, sums, orbits):
    count = applied.shape[0] // orbits
    parts = 4
    return pl.pallas_call(
        finish_kernel,
        out_shape=jax.ShapeDtypeStruct((orbits, count, 128), F32),
        in_specs=[VMEM] * (2 + len(sums)),
        out_specs=pl.BlockSpec(memory_space=pl.ANY),
        scratch_shapes=[
            pltpu.VMEM((parts, count // parts * orbits, 128), F32),
            pltpu.SemaphoreType.DMA((parts, orbits)),
        ],
        compiler_params=params(),
        name="finish",
    )(applied, locked_flat, *sums)


def gram_kernel(locked_ref, flat_ref, gram_ref, wide):
    locked_count, span, lanes = locked_ref.shape
    chunk = 16
    pitch = 3 * chunk + 1
    for c in range(span // chunk):
        for k in range(locked_count):
            value = locked_ref[k, c * chunk : (c + 1) * chunk].astype(F32)
            for g in range(chunk // 8):
                wide[pl.ds(k * pitch + 24 * g, 8, stride=3), :] = value[8 * g : 8 * g + 8]
        for j in range(chunk):
            line = wide[pl.ds(3 * j, locked_count, stride=pitch), :]
            at = c * chunk + j
            flat_ref[:, at * lanes : (at + 1) * lanes] = line.astype(BF16)
    strip = flat_ref[...]
    part = lax.dot_general(strip, strip, NT, preferred_element_type=F32)

    @pl.when(pl.program_id(0) == 0)
    def _():
        gram_ref[...] = part

    @pl.when(pl.program_id(0) > 0)
    def _():
        gram_ref[...] += part


def gram_of(locked):
    locked_count, span_one, span_two, lanes = locked.shape
    count = span_one * span_two
    block = 64
    return pl.pallas_call(
        gram_kernel,
        grid=(count // block,),
        out_shape=(
            jax.ShapeDtypeStruct((locked_count, count * lanes), BF16),
            jax.ShapeDtypeStruct((locked_count, locked_count), F32),
        ),
        in_specs=[pl.BlockSpec((locked_count, block, lanes), lambda t: (0, t, 0))],
        out_specs=(
            pl.BlockSpec((locked_count, block * lanes), lambda t: (0, t)),
            pl.BlockSpec((locked_count, locked_count), lambda t: (0, 0)),
        ),
        scratch_shapes=[pltpu.VMEM((locked_count * 49, lanes), F32)],
        compiler_params=params(),
        cost_estimate=pl.CostEstimate(flops=2**28, bytes_accessed=2**23, transcendentals=0),
        name="gram",
    )(locked.reshape(locked_count, count, lanes))


def on_device(
    orbitals,
    potential,
    locked,
    sphere_cell,
    sphere_owner,
    sphere_atom,
    sphere_profile,
    atom_strength,
    atom_channels,
):
    orbits, span_one, span_two, span_three = orbitals.shape
    locked_count = locked.shape[0]
    atom_slots = atom_channels.shape[3]
    channels, points = sphere_profile.shape[3:]
    classes = min(lax.axis_size("gz"), 3)
    cell, owner, atom = (x.reshape(1, points) for x in (sphere_cell, sphere_owner, sphere_atom))
    cells = span_one * span_two * span_three
    code = (owner * atom_slots + atom) * cells + cell
    profile = sphere_profile.reshape(channels, 1, points)

    rows, table, ends, low, high, left, right = turn(orbitals)
    below = shifted(high, "gx", 1)
    above = shifted(low, "gx", -1)
    before = shifted(right, "gy", 1)
    after = shifted(left, "gy", -1)
    near = shifted(ends, "gz", 1)
    far = near if classes <= 2 else shifted(ends, "gz", -1)

    slots = collect(table, code, profile, classes, atom_slots)
    slots, halos = lax.optimization_barrier((slots, (below, above, before, after, near, far)))
    below, above, before, after, near, far = halos

    if classes == 1:
        parts = merge(slots, 3)
    elif classes == 2:
        parts = merge((slots[0], shifted(slots[1], "gz", 1)), 3)
    else:
        parts = merge((slots[1], shifted(slots[2], "gz", 1), shifted(slots[0], "gz", -1)), 3)
    parts = merge((parts[1], shifted(parts[2], "gx", 1), shifted(parts[0], "gx", -1)), 3)
    active = (
        jnp.arange(channels, dtype=jnp.int32)[None, :]
        < atom_channels.reshape(atom_slots)[:, None]
    )
    strength = jnp.where(active, atom_strength.reshape(atom_slots, channels), 0.0)
    strength = jnp.repeat(strength, orbits, axis=1)
    back = weigh(parts[1], shifted(parts[2], "gy", 1), shifted(parts[0], "gy", -1), strength)

    locked, back = lax.optimization_barrier((locked, back))
    flats = gram_of(locked)
    sides = shifted(back, "gy", 1), shifted(back, "gy", -1)
    sides, (locked_flat, gram) = lax.optimization_barrier((sides, flats))
    back = stack((sides[0], back, sides[1]))
    back, rows = lax.optimization_barrier((back, rows))
    local = stencil(rows, below, above, before, after, near, far, potential)
    sides = shifted(back, "gx", 1), shifted(back, "gx", -1)
    sides, local = lax.optimization_barrier((sides, local))
    back = stack((sides[0], back, sides[1]))
    backs = (back,)
    if classes == 2:
        backs = (back, shifted(back, "gz", 1))
    elif classes == 3:
        backs = (shifted(back, "gz", 1), back, shifted(back, "gz", -1))
    applied, *shares = spread(
        backs, code, profile, local.reshape(-1, span_three), locked_flat, gram, atom_slots
    )
    return finish(applied, locked_flat, summed(shares), orbits).reshape(orbitals.shape)


def solution(mesh):
    placed = (
        P(None, "gx", "gy", "gz"),
        P("gx", "gy", "gz"),
        P(None, "gx", "gy", "gz"),
        P("gx", "gy", "gz", None),
        P("gx", "gy", "gz", None),
        P("gx", "gy", "gz", None),
        P("gx", "gy", "gz", None, None),
        P("gx", "gy", "gz", None, None),
        P("gx", "gy", "gz", None),
    )
    return jax.shard_map(
        on_device, mesh=mesh, in_specs=placed, out_specs=P(None, "gx", "gy", "gz"), check_vma=False
    )
```

```python
import functools

import jax
import jax.numpy as jnp
from jax import lax
from jax.experimental import pallas as pl
from jax.experimental.pallas import tpu as pltpu
from jax.sharding import PartitionSpec as P

STENCIL_WEIGHTS = (-205.0 / 72.0, 8.0 / 5.0, -1.0 / 5.0, 8.0 / 315.0, -1.0 / 560.0)
F32, BF16 = jnp.float32, jnp.bfloat16
NT = (((1,), (1,)), ((), ()))
VMEM = pl.BlockSpec(memory_space=pltpu.VMEM)
MIB = 1024 * 1024
COLLECT_TILE = 4096
SPREAD_TILE = 16384
COLLECT_SUB = 512
SPREAD_SUB = 2048
FLAT = ("gx", "gy")


def params(mebibytes=36):
    return pltpu.CompilerParams(vmem_limit_bytes=mebibytes * MIB)


def shifted(block, axis, step):
    count = lax.axis_size(axis)
    return lax.ppermute(block, axis, [(i, (i + step) % count) for i in range(count)])


def split_pieces(values):
    upper = values.astype(BF16).astype(F32)
    return upper, values - upper


def turn_kernel(orb_ref, rows_ref, table_ref, ends_ref, low_ref, high_ref, left_ref, right_ref):
    span_one, span_two, orbits, lanes = rows_ref.shape
    count = span_one * span_two
    half = count // 2
    lane = lax.broadcasted_iota(jnp.int32, (orbits, lanes), 1)
    packed = [None] * span_one
    for pair in range(half // 2):
        for side in range(2):
            found = []
            for r in (side * half + 2 * pair, side * half + 2 * pair + 1):
                value = orb_ref[pl.ds(r, orbits, stride=count), :]
                i, j = divmod(r, span_two)
                rows_ref[i, j] = value
                if i < 4:
                    low_ref[i, j] = value
                if i >= span_one - 4:
                    high_ref[i + 4 - span_one, j] = value
                if j < 4:
                    left_ref[i, j] = value
                if j >= span_two - 4:
                    right_ref[i, j + 4 - span_two] = value
                found.append(value)
                turned = pltpu.roll(value, (4 + 8 * j) % lanes, 1)
                packed[i] = turned if j == 0 else jnp.where(lane >= 8 * j, turned, packed[i])
                if j == span_two - 1:
                    ends_ref[i] = packed[i]
            upper, lower = split_pieces(jnp.concatenate(found, axis=0))
            low, high = pair * 2 * orbits, (pair + 1) * 2 * orbits
            for piece, base in ((upper, 0), (lower, 256)):
                base = base + side * 128
                table_ref[low:high, base : base + 128] = piece.astype(BF16)


def turn(orbitals):
    orbits, span_one, span_two, lanes = orbitals.shape
    count = span_one * span_two
    return pl.pallas_call(
        turn_kernel,
        out_shape=(
            jax.ShapeDtypeStruct((span_one, span_two, orbits, lanes), F32),
            jax.ShapeDtypeStruct((count // 2 * orbits, 512), BF16),
            jax.ShapeDtypeStruct((span_one, orbits, lanes), F32),
            jax.ShapeDtypeStruct((4, span_two, orbits, lanes), F32),
            jax.ShapeDtypeStruct((4, span_two, orbits, lanes), F32),
            jax.ShapeDtypeStruct((span_one, 4, orbits, lanes), F32),
            jax.ShapeDtypeStruct((span_one, 4, orbits, lanes), F32),
        ),
        in_specs=[VMEM],
        out_specs=(VMEM,) * 7,
        compiler_params=params(),
        cost_estimate=pl.CostEstimate(flops=2**26, bytes_accessed=2**23, transcendentals=0),
        name="turn",
    )(orbitals.reshape(orbits * count, lanes))


def cut(value, count):
    assert count & (count - 1) == 0
    return lax.shift_right_logical(value, jnp.int32(count.bit_length() - 1)), value & (count - 1)


def cell_parts(code, cells, half):
    row, lane = cut(code & (cells - 1), 128)
    group, row = cut(row, half)
    return group, row, lane


def label_parts(code, cells, atom_slots, classes):
    owner, atom = cut(cut(code, cells)[0], atom_slots)
    across = lax.shift_right_logical(owner * 43, jnp.int32(7))
    along = owner - 3 * across
    if classes == 1:
        along = jnp.zeros_like(along)
    elif classes == 2:
        along = jnp.where(along == 1, 0, 1)
    return along * 9 + across, atom


def pair_onehot(outer, outer_count, inner, inner_count, padded=0):
    tile = outer.shape[1]
    rows = lax.broadcasted_iota(jnp.int32, (inner_count, tile), 0)
    block = jnp.where(rows == inner, 1.0, 0.0)
    wide = jnp.broadcast_to(outer, (inner_count, tile))
    parts = [jnp.where(wide == at, block, 0.0) for at in range(outer_count)]
    if padded > outer_count * inner_count:
        parts.append(jnp.zeros((padded - outer_count * inner_count, tile), F32))
    return jnp.concatenate(parts, axis=0).astype(BF16)


def collect_kernel(table_ref, code_ref, profile_ref, *refs, classes, atom_slots):
    out_refs, picked_refs, total = refs[:classes], refs[classes : classes + 2], refs[-1]
    step = pl.program_id(0)
    orbits = 8
    half = table_ref.shape[0] // orbits
    cells = half * 2 * 128
    channels = profile_ref.shape[0]
    subs = COLLECT_TILE // COLLECT_SUB

    def pick(at, target):
        group, _, lane = cell_parts(code_ref[:, pl.ds(pl.multiple_of(at, COLLECT_SUB), COLLECT_SUB)], cells, half)
        spot = pair_onehot(group, 2, lane, 128)
        target[...] = jnp.dot(
            table_ref[...], jnp.concatenate([spot, spot], axis=0), preferred_element_type=F32
        )

    def add(at, picked, live=None):
        here = pl.ds(pl.multiple_of(at, COLLECT_SUB), COLLECT_SUB)
        code = code_ref[:, here]
        wide_row = jnp.broadcast_to(cell_parts(code, cells, half)[1], (orbits, COLLECT_SUB))
        if live is not None:
            wide_row = jnp.where(live, wide_row, half)
        values = jnp.zeros((orbits, COLLECT_SUB), F32)
        for r in range(half):
            values = jnp.where(wide_row == r, picked[r * orbits : (r + 1) * orbits, :], values)
        products = jnp.concatenate(
            [profile_ref[p, :, here] * values for p in range(channels)], axis=0
        )
        pieces = jnp.concatenate(split_pieces(products), axis=0).astype(BF16)
        outer, inner = label_parts(code, cells, atom_slots, classes)
        onehot = pair_onehot(outer, 9 * classes, inner, atom_slots)
        return lax.dot_general(onehot, pieces, NT, preferred_element_type=F32)

    @pl.when(step == 0)
    def _():
        total[...] = jnp.zeros_like(total)

    start = step * COLLECT_TILE
    part = None
    for s in range(subs):
        pick(start + s * COLLECT_SUB, picked_refs[s % 2])
        if s == 0:
            part = add(jnp.maximum(start - COLLECT_SUB, 0), picked_refs[1], step > 0)
        else:
            part = part + add(start + (s - 1) * COLLECT_SUB, picked_refs[(s - 1) % 2])
    total[...] += part

    @pl.when(step == pl.num_programs(0) - 1)
    def _():
        total[...] += add(start + (subs - 1) * COLLECT_SUB, picked_refs[(subs - 1) % 2])
        rows, width = out_refs[0].shape
        for c, out_ref in enumerate(out_refs):
            block = total[c * rows : (c + 1) * rows]
            out_ref[...] = block[:, :width] + block[:, width:]


def collect(table, code, profile, classes, atom_slots):
    points = code.shape[1]
    channels = profile.shape[0]
    rows, width = 9 * atom_slots, channels * 8
    return pl.pallas_call(
        functools.partial(collect_kernel, classes=classes, atom_slots=atom_slots),
        grid=(points // COLLECT_TILE,),
        out_shape=(jax.ShapeDtypeStruct((rows, width), F32),) * classes,
        in_specs=[VMEM] * 3,
        out_specs=(VMEM,) * classes,
        scratch_shapes=[
            pltpu.VMEM((table.shape[0], COLLECT_SUB), F32),
            pltpu.VMEM((table.shape[0], COLLECT_SUB), F32),
            pltpu.VMEM((rows * classes, 2 * width), F32),
        ],
        compiler_params=params(),
        cost_estimate=pl.CostEstimate(
            flops=2 * points * table.shape[0] * 512, bytes_accessed=2**21, transcendentals=0
        ),
        name="collect",
    )(table, code, profile)


def fold_kernel(*refs, rows):
    total = None
    for ref in refs[:-1]:
        for at in range(ref.shape[0] // rows):
            block = ref[at * rows : (at + 1) * rows]
            total = block if total is None else total + block
    for at in range(refs[-1].shape[0] // rows):
        refs[-1][at * rows : (at + 1) * rows] = total


def fold(stacks, rows, copies):
    return pl.pallas_call(
        functools.partial(fold_kernel, rows=rows),
        out_shape=jax.ShapeDtypeStruct((rows * copies, stacks[0].shape[1]), F32),
        in_specs=[VMEM] * len(stacks),
        out_specs=VMEM,
        compiler_params=params(),
        name="fold",
    )(*stacks)


def summed(shares):
    if len(shares) == 1:
        return (lax.psum(shares[0], ("gx", "gy", "gz")),)
    mine, other = shares
    rows = mine.shape[0]
    copies = fold((mine, shifted(other, "gz", 1)), rows, lax.axis_size(FLAT))
    mine = fold((lax.all_to_all(copies, FLAT, 0, 0, tiled=True),), rows, 1)
    return mine, shifted(mine, "gz", 1)


def merge_kernel(*refs, addends):
    total = refs[0][...]
    for ref in refs[1:addends]:
        total = total + ref[...]
    out_refs = refs[addends:]
    rows = out_refs[0].shape[0]
    for at, out_ref in enumerate(out_refs):
        out_ref[...] = total[at * rows : (at + 1) * rows]


def merge(addends, pieces):
    rows, width = addends[0].shape
    return pl.pallas_call(
        functools.partial(merge_kernel, addends=len(addends)),
        out_shape=(jax.ShapeDtypeStruct((rows // pieces, width), F32),) * pieces,
        in_specs=[VMEM] * len(addends),
        out_specs=(VMEM,) * pieces,
        compiler_params=params(),
        name="merge",
    )(*addends)


def weigh_kernel(one_ref, two_ref, three_ref, strength_ref, out_ref):
    out_ref[...] = (one_ref[...] + two_ref[...] + three_ref[...]) * strength_ref[...]


def weigh(one, two, three, strength):
    return pl.pallas_call(
        weigh_kernel,
        out_shape=jax.ShapeDtypeStruct(strength.shape, F32),
        in_specs=[VMEM] * 4,
        out_specs=VMEM,
        compiler_params=params(),
        name="weigh",
    )(one, two, three, strength)


def stack_kernel(*refs):
    rows = refs[0].shape[0]
    for at, ref in enumerate(refs[:-1]):
        refs[-1][at * rows : (at + 1) * rows] = ref[...]


def stack(blocks):
    rows, width = blocks[0].shape
    return pl.pallas_call(
        stack_kernel,
        out_shape=jax.ShapeDtypeStruct((rows * len(blocks), width), F32),
        in_specs=[VMEM] * len(blocks),
        out_specs=VMEM,
        compiler_params=params(),
        name="stack",
    )(*blocks)


def stencil_kernel(rows_ref, below_ref, above_ref, left_ref, right_ref, near_ref, far_ref, pot_ref, out_ref, tall, pair):
    span_one, span_two, orbits, lanes = rows_ref.shape
    rows = span_one * span_two * orbits
    weights = [-0.5 * w for w in STENCIL_WEIGHTS]
    tall[0:4] = below_ref[...]
    tall[4 : 4 + span_one] = rows_ref[...]
    tall[4 + span_one : 8 + span_one] = above_ref[...]
    source = lax.broadcasted_iota(jnp.int32, (lanes, lanes), 0)
    target = lax.broadcasted_iota(jnp.int32, (lanes, lanes), 1)
    ghost = jnp.where(source % 8 < 4, source % 8 - 4, source % 8 - 4 + lanes)

    def band(gap):
        found = jnp.zeros((lanes, lanes), F32)
        for d in range(1, 5):
            found = jnp.where(jnp.abs(gap) == d, weights[d], found)
        return split_pieces(found)

    main_upper, main_lower = band(source - target)
    ends_upper, ends_lower = band(ghost - target)
    ends = jnp.where(source < 16, ends_upper, jnp.where(source < 24, ends_lower, 0.0))
    first = jnp.concatenate([main_upper, main_upper], axis=0).astype(BF16)
    second = jnp.concatenate([main_lower, ends], axis=0).astype(BF16)
    lane = lax.broadcasted_iota(jnp.int32, (orbits, lanes), 1)

    def prepare(i, carry):
        upper, lower = split_pieces(rows_ref[i].reshape(span_two * orbits, lanes))
        base = pl.multiple_of(i * span_two * orbits, span_two * orbits)
        pair[pl.ds(base, span_two * orbits), :lanes] = lower.astype(BF16)
        pair[pl.ds(base, span_two * orbits), lanes : 2 * lanes] = upper.astype(BF16)
        upper, lower = split_pieces(jnp.where(lane % 8 < 4, near_ref[i], far_ref[i]))
        found = []
        for j in range(span_two):
            one = pltpu.roll(upper, (lanes - 8 * j) % lanes, 1)
            two = pltpu.roll(lower, (lanes + 8 - 8 * j) % lanes, 1)
            three = pltpu.roll(upper, (lanes + 16 - 8 * j) % lanes, 1)
            found.append(jnp.where(lane < 8, one, jnp.where(lane < 16, two, three)))
        pair[pl.ds(base, span_two * orbits), 2 * lanes :] = jnp.concatenate(
            found, axis=0
        ).astype(BF16)
        return carry

    lax.fori_loop(0, span_one, prepare, 0)
    along = jnp.dot(pair[:, : 2 * lanes], first, preferred_element_type=F32)
    along = along + jnp.dot(pair[:, lanes:], second, preferred_element_type=F32)
    out_ref[...] = along.reshape(out_ref.shape)

    def plane(i, carry):
        line = [left_ref[i, j] for j in range(4)]
        line += [rows_ref[i, j] for j in range(span_two)]
        line += [right_ref[i, j] for j in range(4)]
        for j in range(span_two):
            acc = out_ref[i, j] + line[4 + j] * (3.0 * weights[0] + pot_ref[i, j : j + 1, :])
            for d in range(1, 5):
                four = tall[i + 4 + d, j] + tall[i + 4 - d, j]
                four = four + (line[4 + j + d] + line[4 + j - d])
                acc = acc + weights[d] * four
            out_ref[i, j] = acc
        return carry

    lax.fori_loop(0, span_one, plane, 0)


def stencil(rows, below, above, left, right, near, far, potential):
    span_one, span_two, orbits, lanes = rows.shape
    return pl.pallas_call(
        stencil_kernel,
        out_shape=jax.ShapeDtypeStruct(rows.shape, F32),
        in_specs=[VMEM] * 8,
        out_specs=VMEM,
        scratch_shapes=[
            pltpu.VMEM((span_one + 8, span_two, orbits, lanes), F32),
            pltpu.VMEM((span_one * span_two * orbits, 3 * lanes), BF16),
        ],
        compiler_params=params(),
        cost_estimate=pl.CostEstimate(flops=2**24, bytes_accessed=2**22, transcendentals=0),
        name="stencil",
    )(rows, below, above, left, right, near, far, potential)


def spread_kernel(*refs, classes, atom_slots):
    back_refs = refs[:classes]
    code_ref, profile_ref, local_ref, locked_ref, gram_ref = refs[classes : classes + 5]
    out_ref, *sums_refs = refs[classes + 5 : -5]
    turned, weights_a, weights_b, total, corr_ref = refs[-5:]
    step = pl.program_id(0)
    orbits = 8
    half = total.shape[0] // orbits
    groups = total.shape[1] // 128
    cells = half * groups * 128
    locked_count = gram_ref.shape[0]
    channels = profile_ref.shape[0]
    width = back_refs[0].shape[1]
    weights = (weights_a, weights_b)
    subs = SPREAD_TILE // SPREAD_SUB

    @pl.when(step == 0)
    def _():
        whole = jnp.concatenate([ref[...] for ref in back_refs], axis=0)
        pad = turned.shape[1] - whole.shape[0]
        whole = jnp.concatenate([whole, jnp.zeros((pad, width), F32)], axis=0)
        whole = jnp.concatenate([whole, jnp.zeros((whole.shape[0], 128 - width), F32)], axis=1)
        flipped = whole.T[:width]
        turned[...] = jnp.concatenate(split_pieces(flipped), axis=0).astype(BF16)
        total[...] = jnp.zeros_like(total)

    def weigh_points(at, target):
        here = pl.ds(at, SPREAD_SUB)
        code = code_ref[:, here]
        outer, inner = label_parts(code, cells, atom_slots, classes)
        onehot = pair_onehot(outer, 9 * classes, inner, atom_slots, turned.shape[1])
        picked = jnp.dot(turned[...], onehot, preferred_element_type=F32)
        spread = jnp.zeros((orbits, SPREAD_SUB), F32)
        for p in range(channels):
            low, high = p * orbits, width + p * orbits
            term = picked[low : low + orbits] + picked[high : high + orbits]
            spread = spread + profile_ref[p, :, here] * term
        upper, lower = split_pieces(spread)
        wide_row = jnp.broadcast_to(cell_parts(code, cells, half)[1], (orbits, SPREAD_SUB))
        for pair in range(half // 2):
            first, second = wide_row == 2 * pair, wide_row == 2 * pair + 1
            for place, piece in enumerate((upper, lower)):
                both = jnp.concatenate(
                    [jnp.where(first, piece, 0.0), jnp.where(second, piece, 0.0)], axis=0
                )
                target[pair * 16 : (pair + 1) * 16, place * SPREAD_SUB : (place + 1) * SPREAD_SUB] = both.astype(BF16)

    def scatter(at, source):
        group, _, lane = cell_parts(code_ref[:, pl.ds(at, SPREAD_SUB)], cells, half)
        spot = pair_onehot(group, groups, lane, 128)
        return lax.dot_general(
            source[...], jnp.concatenate([spot, spot], axis=1), NT, preferred_element_type=F32
        )

    part = None
    for s in range(subs + 1):
        at = step * SPREAD_TILE + s * SPREAD_SUB
        if s < subs:
            weigh_points(pl.multiple_of(at, SPREAD_SUB), weights[s % 2])
        if s > 0:
            term = scatter(pl.multiple_of(at - SPREAD_SUB, SPREAD_SUB), weights[(s - 1) % 2])
            part = term if part is None else part + term
    total[...] += part

    @pl.when(step == pl.num_programs(0) - 1)
    def _():
        rows = half * orbits
        for g in range(groups):
            there = slice(g * rows, (g + 1) * rows)
            out_ref[there] = total[:, g * 128 : (g + 1) * 128] + local_ref[there]
        corr_ref[...] = jnp.zeros_like(corr_ref)
        chunk = 32

        def add(c, carry):
            base = pl.multiple_of(c * chunk * orbits, 128)
            strip = out_ref[pl.ds(base, chunk * orbits), :]
            strip = jnp.concatenate(
                [strip[m * orbits : (m + 1) * orbits] for m in range(chunk)], axis=1
            ).astype(BF16)
            held = locked_ref[:, pl.ds(pl.multiple_of(c * chunk * 128, 128), chunk * 128)]
            corr_ref[...] += lax.dot_general(strip, held, NT, preferred_element_type=F32)
            return carry

        lax.fori_loop(0, groups * half // chunk, add, 0)
        side = locked_count // 2
        corr, gram = corr_ref[...], gram_ref[...]
        rest = jnp.zeros((side - 2 * orbits, side), F32)
        sums = jnp.concatenate(
            [
                gram[:side, :side],
                gram[side:, :side],
                gram[side:, side:],
                jnp.concatenate([corr[:, :side], corr[:, side:], rest], axis=0),
            ],
            axis=1,
        )
        if len(sums_refs) == 1:
            sums_refs[0][...] = sums
        else:
            middle = sums.shape[0] // 2
            first = lax.axis_index("gz") == 0
            sums_refs[0][...] = jnp.where(first, sums[:middle], sums[middle:])
            sums_refs[1][...] = jnp.where(first, sums[middle:], sums[:middle])


def spread(backs, code, profile, local, locked_flat, gram, atom_slots):
    classes = len(backs)
    points = code.shape[1]
    channels = profile.shape[0]
    labels = 9 * classes * atom_slots
    padded = (labels + 127) // 128 * 128
    rows = local.shape[0] // 4
    locked_count = gram.shape[0]
    shares = 2 if classes == 2 else 1
    sums = jax.ShapeDtypeStruct((locked_count // 2 // shares, 2 * locked_count), F32)
    return pl.pallas_call(
        functools.partial(spread_kernel, classes=classes, atom_slots=atom_slots),
        grid=(points // SPREAD_TILE,),
        out_shape=(jax.ShapeDtypeStruct(local.shape, F32),) + (sums,) * shares,
        in_specs=[VMEM] * (classes + 5),
        out_specs=(VMEM,) * (1 + shares),
        scratch_shapes=[
            pltpu.VMEM((2 * channels * 8, padded), BF16),
            pltpu.VMEM((rows, 2 * SPREAD_SUB), BF16),
            pltpu.VMEM((rows, 2 * SPREAD_SUB), BF16),
            pltpu.VMEM((rows, 512), F32),
            pltpu.VMEM((8, locked_count), F32),
        ],
        compiler_params=params(),
        cost_estimate=pl.CostEstimate(
            flops=2 * points * rows * 1024, bytes_accessed=2**23, transcendentals=0
        ),
        name="spread",
    )(*backs, code, profile, local, locked_flat, gram)


def solve_gram(gram):
    size = gram.shape[0]
    wide = (8, 2 * size)
    rows = lax.broadcasted_iota(jnp.int32, (size, size), 0)
    lanes = lax.broadcasted_iota(jnp.int32, (size, size), 1)
    both = jnp.concatenate([jnp.where(rows == lanes, 1.0, 0.0), gram], axis=1)
    blocks = [both[8 * b : 8 * b + 8] for b in range(size // 8)]
    place = lax.broadcasted_iota(jnp.int32, wide, 0)
    scaled = []
    for k in range(0, size, 2):
        b, s = divmod(k, 8)
        last = s + 2 == 8
        one = {
            c: jnp.broadcast_to(blocks[c][:, size + k : size + k + 1], wide)
            for c in range(b, size // 8)
        }
        two = {
            c: jnp.broadcast_to(blocks[c][:, size + k + 1 : size + k + 2], wide)
            for c in range(b, size // 8)
        }
        corner, side, end = one[b][s : s + 1], two[b][s : s + 1], two[b][s + 1 : s + 2]
        first, second = blocks[b][s : s + 1], blocks[b][s + 1 : s + 2]
        factor = 1.0 / (corner * end - side * side)
        upper = (end * first - side * second) * factor
        lower = (corner * second - side * first) * factor
        if s == 0:
            scaled.append(jnp.broadcast_to(upper, wide))
        else:
            scaled[b] = jnp.where(place == s, upper, scaled[b])
        scaled[b] = jnp.where(place == s + 1, lower, scaled[b])
        for c in range(b + 1 if last else b, size // 8):
            amount = one[c] * upper + two[c] * lower
            if c == b:
                amount = jnp.where(place > s + 1, amount, 0.0)
            blocks[c] = blocks[c] - amount
    return jnp.concatenate(blocks, axis=0), jnp.concatenate(scaled, axis=0)


def finish_kernel(applied_ref, locked_ref, *refs):
    *sums_refs, out_ref, lines, sent = refs
    orbits, locked_count = out_ref.shape[0], locked_ref.shape[0]
    parts = sent.shape[0]
    block = out_ref.shape[1] // parts
    sums = sums_refs[0][...]
    if len(sums_refs) == 2:
        first = lax.axis_index("gz") == 0
        other = sums_refs[1][...]
        sums = jnp.concatenate(
            [jnp.where(first, sums, other), jnp.where(first, other, sums)], axis=0
        )
    side = locked_count // 2
    across = sums[:, side : 2 * side]
    corr = sums[:, 3 * side :]
    corr = jnp.concatenate([corr[:orbits], corr[orbits : 2 * orbits]], axis=1)
    gram = jnp.concatenate(
        [
            jnp.concatenate([sums[:, :side], across.T], axis=1),
            jnp.concatenate([across, sums[:, 2 * side : 3 * side]], axis=1),
        ],
        axis=0,
    )
    upper, scaled = solve_gram(gram)
    middle = lax.dot_general(
        corr,
        scaled[:, :locked_count],
        NT,
        precision=lax.Precision.HIGHEST,
        preferred_element_type=F32,
    )
    mixing = jnp.dot(
        middle,
        upper[:, :locked_count],
        precision=lax.Precision.HIGHEST,
        preferred_element_type=F32,
    ).astype(BF16)

    copies = []
    for part in range(parts):
        cells = slice(part * block * 128, (part + 1) * block * 128)
        amount = jnp.dot(mixing, locked_ref[:, cells], preferred_element_type=F32)
        for r in range(block):
            row = part * block + r
            lines[part, pl.ds(r, orbits, stride=block), :] = (
                applied_ref[row * orbits : (row + 1) * orbits, :] - amount[:, r * 128 : (r + 1) * 128]
            )
        for n in range(orbits):
            copy = pltpu.make_async_copy(
                lines.at[part, pl.ds(n * block, block)],
                out_ref.at[n, pl.ds(part * block, block)],
                sent.at[part, n],
            )
            copy.start()
            copies.append(copy)
    for copy in copies:
        copy.wait()


def finish(applied, locked_flat, sums, orbits):
    count = applied.shape[0] // orbits
    parts = 4
    return pl.pallas_call(
        finish_kernel,
        out_shape=jax.ShapeDtypeStruct((orbits, count, 128), F32),
        in_specs=[VMEM] * (2 + len(sums)),
        out_specs=pl.BlockSpec(memory_space=pl.ANY),
        scratch_shapes=[
            pltpu.VMEM((parts, count // parts * orbits, 128), F32),
            pltpu.SemaphoreType.DMA((parts, orbits)),
        ],
        compiler_params=params(),
        name="finish",
    )(applied, locked_flat, *sums)


def gram_kernel(locked_ref, flat_ref, gram_ref, wide):
    locked_count, span, lanes = locked_ref.shape
    chunk = 16
    pitch = 3 * chunk + 1
    for c in range(span // chunk):
        for k in range(locked_count):
            value = locked_ref[k, c * chunk : (c + 1) * chunk].astype(F32)
            for g in range(chunk // 8):
                wide[pl.ds(k * pitch + 24 * g, 8, stride=3), :] = value[8 * g : 8 * g + 8]
        for j in range(chunk):
            line = wide[pl.ds(3 * j, locked_count, stride=pitch), :]
            at = c * chunk + j
            flat_ref[:, at * lanes : (at + 1) * lanes] = line.astype(BF16)
    strip = flat_ref[...]
    part = lax.dot_general(strip, strip, NT, preferred_element_type=F32)

    @pl.when(pl.program_id(0) == 0)
    def _():
        gram_ref[...] = part

    @pl.when(pl.program_id(0) > 0)
    def _():
        gram_ref[...] += part


def gram_of(locked):
    locked_count, span_one, span_two, lanes = locked.shape
    count = span_one * span_two
    block = 64
    return pl.pallas_call(
        gram_kernel,
        grid=(count // block,),
        out_shape=(
            jax.ShapeDtypeStruct((locked_count, count * lanes), BF16),
            jax.ShapeDtypeStruct((locked_count, locked_count), F32),
        ),
        in_specs=[pl.BlockSpec((locked_count, block, lanes), lambda t: (0, t, 0))],
        out_specs=(
            pl.BlockSpec((locked_count, block * lanes), lambda t: (0, t)),
            pl.BlockSpec((locked_count, locked_count), lambda t: (0, 0)),
        ),
        scratch_shapes=[pltpu.VMEM((locked_count * 49, lanes), F32)],
        compiler_params=params(),
        cost_estimate=pl.CostEstimate(flops=2**28, bytes_accessed=2**23, transcendentals=0),
        name="gram",
    )(locked.reshape(locked_count, count, lanes))


def on_device(
    orbitals,
    potential,
    locked,
    sphere_cell,
    sphere_owner,
    sphere_atom,
    sphere_profile,
    atom_strength,
    atom_channels,
):
    orbits, span_one, span_two, span_three = orbitals.shape
    locked_count = locked.shape[0]
    atom_slots = atom_channels.shape[3]
    channels, points = sphere_profile.shape[3:]
    classes = min(lax.axis_size("gz"), 3)
    cell, owner, atom = (x.reshape(1, points) for x in (sphere_cell, sphere_owner, sphere_atom))
    cells = span_one * span_two * span_three
    code = (owner * atom_slots + atom) * cells + cell
    profile = sphere_profile.reshape(channels, 1, points)

    rows, table, ends, low, high, left, right = turn(orbitals)
    below = shifted(high, "gx", 1)
    above = shifted(low, "gx", -1)
    before = shifted(right, "gy", 1)
    after = shifted(left, "gy", -1)
    near = shifted(ends, "gz", 1)
    far = near if classes <= 2 else shifted(ends, "gz", -1)

    slots = collect(table, code, profile, classes, atom_slots)
    slots, halos = lax.optimization_barrier((slots, (below, above, before, after, near, far)))
    below, above, before, after, near, far = halos

    if classes == 1:
        parts = merge(slots, 3)
    elif classes == 2:
        parts = merge((slots[0], shifted(slots[1], "gz", 1)), 3)
    else:
        parts = merge((slots[1], shifted(slots[2], "gz", 1), shifted(slots[0], "gz", -1)), 3)
    parts = merge((parts[1], shifted(parts[2], "gx", 1), shifted(parts[0], "gx", -1)), 3)
    active = (
        jnp.arange(channels, dtype=jnp.int32)[None, :]
        < atom_channels.reshape(atom_slots)[:, None]
    )
    strength = jnp.where(active, atom_strength.reshape(atom_slots, channels), 0.0)
    strength = jnp.repeat(strength, orbits, axis=1)
    back = weigh(parts[1], shifted(parts[2], "gy", 1), shifted(parts[0], "gy", -1), strength)

    locked, back = lax.optimization_barrier((locked, back))
    flats = gram_of(locked)
    sides = shifted(back, "gy", 1), shifted(back, "gy", -1)
    sides, (locked_flat, gram) = lax.optimization_barrier((sides, flats))
    back = stack((sides[0], back, sides[1]))
    back, rows = lax.optimization_barrier((back, rows))
    local = stencil(rows, below, above, before, after, near, far, potential)
    sides = shifted(back, "gx", 1), shifted(back, "gx", -1)
    sides, local = lax.optimization_barrier((sides, local))
    back = stack((sides[0], back, sides[1]))
    backs = (back,)
    if classes == 2:
        backs = (back, shifted(back, "gz", 1))
    elif classes == 3:
        backs = (shifted(back, "gz", 1), back, shifted(back, "gz", -1))
    applied, *shares = spread(
        backs, code, profile, local.reshape(-1, span_three), locked_flat, gram, atom_slots
    )
    return finish(applied, locked_flat, summed(shares), orbits).reshape(orbitals.shape)


def solution(mesh):
    placed = (
        P(None, "gx", "gy", "gz"),
        P("gx", "gy", "gz"),
        P(None, "gx", "gy", "gz"),
        P("gx", "gy", "gz", None),
        P("gx", "gy", "gz", None),
        P("gx", "gy", "gz", None),
        P("gx", "gy", "gz", None, None),
        P("gx", "gy", "gz", None, None),
        P("gx", "gy", "gz", None),
    )
    return jax.shard_map(
        on_device, mesh=mesh, in_specs=placed, out_specs=P(None, "gx", "gy", "gz"), check_vma=False
    )
```
